512 devices in a mesh: section: 2 (over core), row: 16 (over y, x), col: 16 (over z).
Axes of the slice: x: 4, y: 4, z: 16, core: 2. Of those that a mesh axis runs over, the one named last changes fastest.
Arguments:
- features: bfloat16 [2, 64, 128, 2048], P(None, None, 'row', 'col'), may hold values from -6 to 6
- prop_input: bfloat16 [2, 64, 128, 3, 3], P('section'), may hold values from -0.1875 to 0.1875
- prop_middle: bfloat16 [2, 64, 64, 3, 3], P('section'), may hold values from -0.25 to 0.25
- prop_output: bfloat16 [2, 64, 64, 3, 3], P('section'), may hold values from -0.25 to 0.25
- merge_weight: bfloat16 [64, 128, 3, 3], replicated, may hold values from -0.1875 to 0.1875
- first_weight: bfloat16 [64, 64, 3, 3], replicated, may hold values from -0.25 to 0.25
- second_weight: bfloat16 [64, 64, 3, 3], replicated, may hold values from -0.25 to 0.25
- head_weight: bfloat16 [48, 64, 3, 3], replicated, may hold values from -0.25 to 0.25
- cotangent: bfloat16 [2, 3, 512, 8192], P('section', None, 'row', 'col'), may hold values from -6 to 6
Outputs:
- upscaled: float32 [2, 3, 512, 8192], P('section', None, 'row', 'col')
- adjoint: float32 [2, 128, 128, 2048], P('section', None, 'row', 'col')
The draws below stay inside these ranges and needn't reach their ends.
All inputs are finite; a program needn't handle non-finite values.
Results may differ from the reference program's by a relative error of at most 0.015.
Values may be sent and summed in bfloat16 or wider, within the bound.
A program may use at most 64 MiB of HBM per device.

```python
import jax
import jax.numpy as jnp
from jax import lax

CH = 64
SCALE = 4
FRAMES = 2
NH = 128
NW = 2048


def steps_of(key, shape, split, low, high):
    def one(position, blocks):
        draws = jax.random.uniform(jax.random.fold_in(jax.random.fold_in(key, 6), position), (blocks,), jnp.float32, low / len(split), high / len(split))
        return jnp.repeat(jnp.exp(draws), shape[position] // blocks).reshape((-1,) + (1,) * (len(shape) - position - 1))

    factor_of = one(*split[0])
    for cut in split[1:]:
        factor_of = factor_of * one(*cut)
    return factor_of


def gaussian(key, extent, scale, reach, split=(), kind=jnp.bfloat16):
    result = jax.random.normal(key, extent, jnp.float32) * scale
    if len(split) > 0:
        result = steps_of(key, extent, split, -0.22, 0.18) * result
    return jnp.clip(result, min=-reach, max=reach).astype(kind)


def setup_inputs(seed: int = 0) -> dict:
    keys = jax.random.split(jax.random.key(seed), 10)
    return {
        "features": gaussian(keys[0], (FRAMES, CH, NH, NW), 1.0, 6.0, ((2, 16), (3, 16))),
        "prop_input": gaussian(keys[1], (2, CH, 2 * CH, 3, 3), (18 * CH) ** -0.5, 0.1875, ((0, 2),)),
        "prop_middle": gaussian(keys[2], (2, CH, CH, 3, 3), (9 * CH) ** -0.5, 0.25, ((0, 2),)),
        "prop_output": gaussian(keys[3], (2, CH, CH, 3, 3), (9 * CH) ** -0.5, 0.25, ((0, 2),)),
        "merge_weight": gaussian(keys[4], (CH, 2 * CH, 3, 3), (18 * CH) ** -0.5, 0.1875),
        "first_weight": gaussian(keys[5], (CH, CH, 3, 3), (9 * CH) ** -0.5, 0.25),
        "second_weight": gaussian(keys[6], (CH, CH, 3, 3), (9 * CH) ** -0.5, 0.25),
        "head_weight": gaussian(keys[7], (3 * SCALE * SCALE, CH, 3, 3), (9 * CH) ** -0.5, 0.25),
        "cotangent": gaussian(keys[8], (FRAMES, 3, SCALE * NH, SCALE * NW), 1.0, 6.0, ((0, 2), (2, 16), (3, 16))),
    }


def conv_same(weight, source):
    return lax.conv_general_dilated(source, weight, (1, 1), ((1, 1), (1, 1)), dimension_numbers=("NCHW", "OIHW", "NCHW"), preferred_element_type=jnp.float32)


def flipped(weight):
    return jnp.transpose(weight[:, :, ::-1, ::-1], (1, 0, 2, 3))


def leaky_relu(signal):
    return jnp.where(signal > 0, signal, 0.1 * signal)


def silu_slope(signal):
    sigma = jax.nn.sigmoid(signal)
    return sigma * (1.0 + signal * (1.0 - sigma))


def propagate(features, prop_input, prop_middle, prop_output, visit_order):
    hidden_state = jnp.zeros((1, CH, NH, NW), jnp.bfloat16)
    kept_states = [None] * FRAMES
    for frame_at in visit_order:
        joined = jnp.concatenate([features[frame_at:frame_at + 1], hidden_state], axis=1)
        lifted = leaky_relu(conv_same(prop_input, joined)).astype(jnp.bfloat16)
        inner_act = jax.nn.relu(conv_same(prop_middle, lifted)).astype(jnp.bfloat16)
        hidden_state = (lifted.astype(jnp.float32) + conv_same(prop_output, inner_act)).astype(jnp.bfloat16)
        kept_states[frame_at] = hidden_state
    return jnp.concatenate(kept_states, axis=0)


def reconstruct(joined, cotangent, merge_weight, first_weight, second_weight, head_weight):
    merged_pre = conv_same(merge_weight, joined)
    merged_act = jax.nn.silu(merged_pre).astype(jnp.bfloat16)
    inner_pre = conv_same(first_weight, merged_act)
    inner_act = jax.nn.silu(inner_pre).astype(jnp.bfloat16)
    refined = (merged_act.astype(jnp.float32) + conv_same(second_weight, inner_act)).astype(jnp.bfloat16)
    head_out = conv_same(head_weight, refined)
    grouped = head_out.reshape(1, 3, SCALE, SCALE, NH, NW)
    upscaled = jnp.transpose(grouped, (0, 1, 4, 2, 5, 3)).reshape(1, 3, NH * SCALE, NW * SCALE)
    back_grouped = cotangent.reshape(1, 3, NH, SCALE, NW, SCALE)
    back_head = jnp.transpose(back_grouped, (0, 1, 3, 5, 2, 4)).reshape(1, 3 * SCALE * SCALE, NH, NW)
    grad_refined = conv_same(flipped(head_weight), back_head).astype(jnp.bfloat16)
    grad_inner = (conv_same(flipped(second_weight), grad_refined) * silu_slope(inner_pre)).astype(jnp.bfloat16)
    grad_merged = grad_refined.astype(jnp.float32) + conv_same(flipped(first_weight), grad_inner)
    grad_pre = (grad_merged * silu_slope(merged_pre)).astype(jnp.bfloat16)
    adjoint = conv_same(flipped(merge_weight), grad_pre)
    return upscaled, adjoint


def reference(features, prop_input, prop_middle, prop_output, merge_weight, first_weight, second_weight, head_weight, cotangent):
    backward_states = propagate(features, prop_input[0], prop_middle[0], prop_output[0], range(FRAMES - 1, -1, -1))
    forward_states = propagate(features, prop_input[1], prop_middle[1], prop_output[1], range(FRAMES))
    upscaled_list = []
    adjoint_list = []
    for frame_at in range(FRAMES):
        joined = jnp.concatenate([backward_states[frame_at:frame_at + 1], forward_states[frame_at:frame_at + 1]], axis=1)
        upscaled, adjoint = reconstruct(joined, cotangent[frame_at:frame_at + 1], merge_weight, first_weight, second_weight, head_weight)
        upscaled_list.append(upscaled)
        adjoint_list.append(adjoint)
    return jnp.concatenate(upscaled_list, axis=0), jnp.concatenate(adjoint_list, axis=0)
```

```python
import functools

import jax
import jax.numpy as jnp
from jax import lax
from jax.experimental import pallas as pl
from jax.experimental.pallas import tpu as pltpu
from jax.sharding import PartitionSpec as P

F32 = jnp.float32
BF16 = jnp.bfloat16
MESH = pl.DeviceIdType.MESH

RIM = 16
COLS = 128
WIDE = COLS + 2 * RIM
OWN = 4
PAIR = 128

AROUND = tuple((dr, dc) for dr in (-1, 0, 1) for dc in (-1, 0, 1) if (dr, dc) != (0, 0))

EX_FIRST, EX_SECOND, EX_COT, EX_STATE1, EX_STATE2 = range(5)


def iota(shape, dim):
    return lax.broadcasted_iota(jnp.int32, shape, dim)


def one_hot(cond):
    return jnp.where(cond, 1.0, 0.0).astype(F32)


def low_lanes(shape):
    return iota(shape, len(shape) - 1) < 64


def kernel(
    rows,
    cols,
    feat,
    w_input,
    w_middle,
    w_output,
    w_merge,
    w_first,
    w_second,
    w_head,
    cot,
    up_out,
    adj_out,
    feat_v,
    w_input_v,
    w_middle_v,
    w_output_v,
    w_merge_v,
    w_first_v,
    w_second_v,
    w_head_v,
    cot_v,
    stage,
    xf1,
    xf2,
    xo2,
    cb,
    s1,
    s2,
    e1,
    lift1,
    inner1,
    state1,
    lift2,
    inner2,
    merged,
    slope_m,
    rec_inner,
    refined,
    grad_ref,
    grad_in_pre,
    grad_in,
    grad_pre,
    k_feat,
    k_state,
    k_middle,
    k_output,
    k_merge2,
    k_merge1,
    k_first,
    k_second,
    k_head,
    k_head_t,
    k_second_t,
    k_first_t,
    k_merge_t,
    head_rows,
    shuffle,
    z_hi,
    z_lo,
    up_v,
    adj_v,
    col_mask,
    load_sem,
    store_sem,
    send_sem,
    recv_sem,
):
    sec = lax.axis_index("section")
    row = lax.axis_index("row")
    col = lax.axis_index("col")
    other = 1 - sec
    first_frame = 1 - sec
    second_frame = sec

    loads = []

    def load(source, target):
        copy = pltpu.make_async_copy(source, target, load_sem.at[len(loads)])
        copy.start()
        loads.append(copy)
        return copy

    load_f1 = load(feat.at[first_frame], feat_v.at[0])
    load_f2 = load(feat.at[second_frame], feat_v.at[1])
    load_cot = load(cot, cot_v)
    load_prop = [load(w_input, w_input_v), load(w_middle, w_middle_v), load(w_output, w_output_v)]
    load_head = load(w_head, w_head_v)
    load_second = load(w_second, w_second_v)
    load_merge = load(w_merge, w_merge_v)
    load_first = load(w_first, w_first_v)

    barrier = pltpu.get_barrier_semaphore()

    def place(dr, dc, section):
        return (section, lax.rem(row + dr + rows, rows), lax.rem(col + dc + cols, cols))

    partners = [place(dr, dc, s) for dr, dc in AROUND for s in (sec, other)] + [(other, row, col)]
    for partner in partners:
        pl.semaphore_signal(barrier, inc=1, device_id=partner, device_id_type=MESH)

    def exchange(kind, src, src_pair, src_col, dst, halo, section):
        copies = []
        for k, (dr, dc) in enumerate(AROUND):
            sp, n, dp = {-1: (0, halo, halo + OWN), 0: (0, OWN, halo), 1: (OWN - halo, halo, 0)}[dr]
            sc, m, dcol = {
                -1: (0, RIM, RIM + COLS),
                0: (0, COLS, RIM),
                1: (COLS - RIM, RIM, 0),
            }[dc]
            copies.append(
                pltpu.make_async_remote_copy(
                    src_ref=src.at[pl.ds(src_pair + sp, n), pl.ds(src_col + sc, m), :],
                    dst_ref=dst.at[pl.ds(dp, n), pl.ds(dcol, m), :],
                    send_sem=send_sem.at[kind, k],
                    recv_sem=recv_sem.at[kind, k],
                    device_id=place(dr, dc, section),
                    device_id_type=MESH,
                )
            )
        return copies

    def clear_outside(buf, halo):
        pairs = buf.shape[0]

        @pl.when(row == 0)
        def _():
            buf[pl.ds(0, halo)] = jnp.zeros((halo, WIDE, PAIR), BF16)

        @pl.when(row == rows - 1)
        def _():
            buf[pl.ds(halo + OWN, halo)] = jnp.zeros((halo, WIDE, PAIR), BF16)

        @pl.when(col == 0)
        def _():
            buf[:, pl.ds(0, RIM), :] = jnp.zeros((pairs, RIM, PAIR), BF16)

        @pl.when(col == cols - 1)
        def _():
            buf[:, pl.ds(RIM + COLS, RIM), :] = jnp.zeros((pairs, RIM, PAIR), BF16)

    def turn_features(at, dst, halo):
        stage[...] = feat_v[at].astype(F32)
        for p in range(OWN):
            two = jnp.concatenate(
                [stage[pl.ds(2 * p + r, 64, stride=8), :] for r in range(2)], axis=0
            )
            dst[halo + p, pl.ds(RIM, COLS), :] = two.T.astype(BF16)

    load_f1.wait()
    turn_features(0, xf1, 3)
    pl.semaphore_wait(barrier, len(partners))
    ex_first = exchange(EX_FIRST, xf1, 3, RIM, xf1, 3, sec)
    for copy in ex_first:
        copy.start()
    load_f2.wait()
    turn_features(1, xf2, 2)
    ex_second = exchange(EX_SECOND, xf2, 2, RIM, xf2, 2, sec)
    for copy in ex_second:
        copy.start()

    k_at, n_at = iota((512, 512), 0), iota((512, 512), 1)
    shuffle[...] = one_hot(n_at == 4 * (k_at & 127) + (k_at >> 7)).astype(BF16)
    m_at, n_at = iota((128, 96), 0), iota((128, 96), 1)
    spread = one_hot(
        (((n_at >> 2) & 7) == (m_at >> 4)) & (((n_at >> 5) * 4 + (n_at & 3)) == (m_at & 15))
    ).astype(BF16)
    load_cot.wait()
    spaced = jnp.dot(spread, cot_v[...], preferred_element_type=F32).astype(BF16)
    parted = lax.dot_general(
        spaced, shuffle[...], (((1,), (1,)), ((), ())), preferred_element_type=F32
    )
    for p in range(OWN):
        pieces = [
            parted[(2 * p + r) * 16 : (2 * p + r + 1) * 16, j * 128 : (j + 1) * 128]
            for r in range(2)
            for j in range(4)
        ]
        cb[2 + p, pl.ds(RIM, COLS), :] = jnp.concatenate(pieces, axis=0).T.astype(BF16)
    ex_cot = exchange(EX_COT, cb, 2, RIM, cb, 2, sec)
    for copy in ex_cot:
        copy.start()

    col_at = iota((WIDE, PAIR), 0) - RIM + col * COLS
    col_mask[...] = one_hot((col_at >= 0) & (col_at < cols * COLS))

    def pack_forward(tap, targets):
        empty = jnp.zeros(tap(0, 0).shape, F32)
        for b in range(3):
            for q in range(4):
                upper = tap(q, b) if q < 3 else empty
                lower = tap(q - 1, b) if q > 0 else empty
                turned = jnp.concatenate([upper, lower], axis=0).T.astype(BF16)
                for t, target in enumerate(targets):
                    target[q * 64 : (q + 1) * 64, b * 128 : (b + 1) * 128] = turned[
                        t * 64 : (t + 1) * 64
                    ]

    def pack_transposed(tap, target):
        width = tap(0, 0).shape[1]
        empty = jnp.zeros((64, width), F32)
        for b in range(3):
            for q in range(4):
                left = tap(q, b) if q < 3 else empty
                right = tap(q - 1, b) if q > 0 else empty
                target[q * 64 : (q + 1) * 64, b * 2 * width : (b + 1) * 2 * width] = (
                    jnp.concatenate([left, right], axis=1).astype(BF16)
                )

    for copy in load_prop:
        copy.wait()
    pack_forward(lambda a, b: w_input_v[a, b].astype(F32), (k_feat, k_state))
    pack_forward(lambda a, b: w_middle_v[a, b].astype(F32), (k_middle,))
    pack_forward(lambda a, b: w_output_v[a, b].astype(F32), (k_output,))

    def conv(sources, matrices, j):
        total = None
        for source, matrix in zip(sources, matrices):
            x = jnp.concatenate([source[j], source[j + 1]], axis=1)
            y = jnp.dot(x, matrix[...], preferred_element_type=F32)
            total = y if total is None else total + y
        w = total.shape[1] // 3
        return (
            total[:, w : 2 * w]
            + pltpu.roll(total[:, :w], 1, 0)
            + pltpu.roll(total[:, 2 * w :], WIDE - 1, 0)
        )

    def inside(start):
        at = row * (2 * OWN) + start + jnp.where(low_lanes((1, PAIR)), 0, 1)
        return col_mask[...] * one_hot((at >= 0) & (at < rows * 2 * OWN))

    def lrelu(v):
        return jnp.where(v > 0, v, 0.1 * v)

    def realign(upper_of, lower_of):
        mixed = jnp.where(
            low_lanes(upper_of.shape), lower_of.astype(F32), upper_of.astype(F32)
        )
        return pltpu.roll(mixed, 64, 1).astype(BF16)

    for copy in ex_first:
        copy.wait_recv()
    clear_outside(xf1, 3)
    for j in range(9):
        v = conv((xf1,), (k_feat,), j)
        lift1[j] = (lrelu(v) * inside(2 * j - 5)).astype(BF16)
    for j in range(8):
        v = conv((lift1,), (k_middle,), j)
        inner1[j] = (jnp.maximum(v, 0.0) * inside(2 * j - 4)).astype(BF16)
    for j in range(7):
        v = conv((inner1,), (k_output,), j) + lift1[j + 1].astype(F32)
        state1[j] = (v * inside(2 * j - 3)).astype(BF16)
    for p in range(OWN):
        e1[p] = realign(
            state1[p + 1, pl.ds(RIM, COLS), :], state1[p + 2, pl.ds(RIM, COLS), :]
        )
    ex_state1 = exchange(EX_STATE1, e1, 0, 0, s1, 2, other)
    ex_state1.append(
        pltpu.make_async_remote_copy(
            src_ref=e1,
            dst_ref=s1.at[pl.ds(2, OWN), pl.ds(RIM, COLS), :],
            send_sem=send_sem.at[EX_STATE1, 8],
            recv_sem=recv_sem.at[EX_STATE1, 8],
            device_id=(other, row, col),
            device_id_type=MESH,
        )
    )
    for copy in ex_state1:
        copy.start()

    for copy in ex_second:
        copy.wait_recv()
    clear_outside(xf2, 2)
    for j in range(7):
        xo2[j] = realign(xf2[j], xf2[j + 1])
    for j in range(6):
        v = conv((xo2, state1), (k_feat, k_state), j)
        lift2[j] = (lrelu(v) * inside(2 * j - 2)).astype(BF16)
    for j in range(5):
        v = conv((lift2,), (k_middle,), j)
        inner2[j] = (jnp.maximum(v, 0.0) * inside(2 * j - 1)).astype(BF16)
    for j in range(4):
        v = conv((inner2,), (k_output,), j) + lift2[j + 1].astype(F32)
        s2[2 + j, pl.ds(RIM, COLS), :] = v[RIM : RIM + COLS].astype(BF16)
    ex_state2 = exchange(EX_STATE2, s2, 2, RIM, s2, 2, sec)
    for copy in ex_state2:
        copy.start()

    load_head.wait()
    m_at, n_at = iota((64, 48), 0), iota((64, 48), 1)
    order = one_hot((n_at == (m_at & 15) * 4 + (m_at >> 4)) & ((m_at & 15) < 12)).astype(BF16)
    for a in range(3):
        for b in range(3):
            head_rows[a, b] = jnp.dot(order, w_head_v[a, b], preferred_element_type=F32)
    pack_transposed(lambda a, b: head_rows[2 - a, 2 - b], k_head_t)
    load_second.wait()
    pack_transposed(lambda a, b: w_second_v[2 - a, 2 - b].astype(F32), k_second_t)

    for copy in ex_cot:
        copy.wait_recv()
    clear_outside(cb, 2)
    for j in range(7):
        v = conv((cb,), (k_head_t,), j)
        grad_ref[j] = (v * inside(2 * j - 3)).astype(BF16)
    for j in range(6):
        grad_in_pre[j] = conv((grad_ref,), (k_second_t,), j) * inside(2 * j - 2)

    load_merge.wait()

    @pl.when(sec == 0)
    def _():
        pack_forward(lambda a, b: w_merge_v[a, b].astype(F32), (k_merge2, k_merge1))

    @pl.when(sec == 1)
    def _():
        pack_forward(lambda a, b: w_merge_v[a, b].astype(F32), (k_merge1, k_merge2))

    load_first.wait()
    pack_forward(lambda a, b: w_first_v[a, b].astype(F32), (k_first,))
    pack_forward(lambda a, b: w_second_v[a, b].astype(F32), (k_second,))
    pack_forward(lambda a, b: head_rows[a, b], (k_head,))
    pack_transposed(lambda a, b: w_first_v[2 - a, 2 - b].astype(F32), k_first_t)
    pack_transposed(lambda a, b: w_merge_v[2 - a, 2 - b].astype(F32), k_merge_t)

    for copy in ex_state1:
        copy.wait_recv()
    clear_outside(s1, 2)
    for copy in ex_state2:
        copy.wait_recv()
    clear_outside(s2, 2)
    for j in range(7):
        v = conv((s1, s2), (k_merge1, k_merge2), j)
        sigma = jax.nn.sigmoid(v)
        merged[j] = (v * sigma * inside(2 * j - 3)).astype(BF16)
        if 1 <= j <= 5:
            slope_m[j - 1] = sigma * (1.0 + v * (1.0 - sigma)) * inside(2 * j - 3)
    for j in range(6):
        v = conv((merged,), (k_first,), j)
        sigma = jax.nn.sigmoid(v)
        rec_inner[j] = (v * sigma * inside(2 * j - 2)).astype(BF16)
        grad_in[j] = (grad_in_pre[j] * (sigma * (1.0 + v * (1.0 - sigma)))).astype(BF16)
    for j in range(5):
        v = conv((rec_inner,), (k_second,), j) + merged[j + 1].astype(F32)
        refined[j] = (v * inside(2 * j - 1)).astype(BF16)
    for j in range(4):
        v = conv((refined,), (k_head,), j)[RIM : RIM + COLS].T
        high = v.astype(BF16)
        low = (v - high.astype(F32)).astype(BF16)
        for r in range(2):
            for i in range(4):
                piece = slice((r * 4 + i) * 16, (r * 4 + i + 1) * 16)
                at = (slice((2 * j + r) * 16, (2 * j + r + 1) * 16), slice(i * 128, (i + 1) * 128))
                z_hi[at] = high[piece]
                z_lo[at] = low[piece]
    m_at, n_at = iota((96, 128), 0), iota((96, 128), 1)
    gather = one_hot(
        (((m_at >> 2) & 7) == (n_at >> 4)) & (((m_at >> 5) * 4 + (m_at & 3)) == (n_at & 15))
    ).astype(BF16)
    total = None
    for z in (z_hi, z_lo):
        ordered = jnp.dot(gather, z[...], preferred_element_type=F32).astype(BF16)
        part = jnp.dot(ordered, shuffle[...], preferred_element_type=F32)
        total = part if total is None else total + part
    up_v[...] = total
    store_up = pltpu.make_async_copy(up_v, up_out, store_sem.at[0])
    store_up.start()

    for j in range(5):
        v = conv((grad_in,), (k_first_t,), j) + grad_ref[j + 1].astype(F32)
        grad_pre[j] = (v * slope_m[j]).astype(BF16)
    for j in range(4):
        v = conv((grad_pre,), (k_merge_t,), j)
        for r in range(2):
            adj_v[pl.ds(2 * j + r, 128, stride=8), :] = v[
                RIM : RIM + COLS, r * 128 : (r + 1) * 128
            ].T
    store_adj = pltpu.make_async_copy(adj_v, adj_out, store_sem.at[1])
    store_adj.start()

    for copies in (ex_first, ex_second, ex_cot, ex_state1, ex_state2):
        for copy in copies:
            copy.wait_send()
    store_up.wait()
    store_adj.wait()


def on_device(
    rows,
    cols,
    features,
    prop_input,
    prop_middle,
    prop_output,
    merge_weight,
    first_weight,
    second_weight,
    head_weight,
    cotangent,
):
    def taps(weight):
        return jnp.transpose(weight, (2, 3, 0, 1))

    def vmem(*shape, dtype=BF16):
        return pltpu.VMEM(shape, dtype)

    def act(pairs, dtype=BF16):
        return pltpu.VMEM((pairs, WIDE, PAIR), dtype)

    scratch = (
        [
            vmem(2, 512, 128),
            vmem(3, 3, 64, 128),
            vmem(3, 3, 64, 64),
            vmem(3, 3, 64, 64),
            vmem(3, 3, 64, 128),
            vmem(3, 3, 64, 64),
            vmem(3, 3, 64, 64),
            vmem(3, 3, 48, 64),
            vmem(96, 512),
            vmem(512, 128, dtype=F32),
            act(10),
            act(8),
            act(7),
            act(8),
            act(8),
            act(8),
            vmem(OWN, COLS, PAIR),
            act(9),
            act(8),
            act(7),
            act(6),
            act(5),
            act(7),
            act(5, F32),
            act(6),
            act(5),
            act(7),
            act(6, F32),
            act(6),
            act(5),
        ]
        + [vmem(256, 384) for _ in range(12)]
        + [
            vmem(256, 768),
            vmem(3, 3, 64, 64, dtype=F32),
            vmem(512, 512),
            vmem(128, 512),
            vmem(128, 512),
            vmem(96, 512, dtype=F32),
            vmem(1024, 128, dtype=F32),
            vmem(WIDE, PAIR, dtype=F32),
            pltpu.SemaphoreType.DMA((10,)),
            pltpu.SemaphoreType.DMA((2,)),
            pltpu.SemaphoreType.DMA((5, 9)),
            pltpu.SemaphoreType.DMA((5, 9)),
        ]
    )
    up, adj = pl.pallas_call(
        functools.partial(kernel, rows, cols),
        out_shape=(
            jax.ShapeDtypeStruct((96, 512), F32),
            jax.ShapeDtypeStruct((1024, 128), F32),
        ),
        in_specs=[pl.BlockSpec(memory_space=pl.ANY)] * 9,
        out_specs=(pl.BlockSpec(memory_space=pl.ANY), pl.BlockSpec(memory_space=pl.ANY)),
        scratch_shapes=scratch,
        compiler_params=pltpu.CompilerParams(
            collective_id=0, has_side_effects=True, vmem_limit_bytes=48 * 1024 * 1024
        ),
    )(
        features.reshape(2, 512, 128),
        taps(prop_input[0]),
        taps(prop_middle[0]),
        taps(prop_output[0]),
        taps(merge_weight),
        taps(first_weight),
        taps(second_weight),
        taps(head_weight),
        cotangent.reshape(96, 512),
    )
    return up.reshape(1, 3, 32, 512), adj.reshape(1, 128, 8, 128)


def solution(mesh):
    rows, cols = mesh.shape["row"], mesh.shape["col"]
    placed = (
        P(None, None, "row", "col"),
        P("section", None, None, None, None),
        P("section", None, None, None, None),
        P("section", None, None, None, None),
        P(),
        P(),
        P(),
        P(),
        P("section", None, "row", "col"),
    )
    return jax.shard_map(
        functools.partial(on_device, rows, cols),
        mesh=mesh,
        in_specs=placed,
        out_specs=(P("section", None, "row", "col"), P("section", None, "row", "col")),
        check_vma=False,
    )
```

```python
import functools

import jax
import jax.numpy as jnp
from jax import lax
from jax.experimental import pallas as pl
from jax.experimental.pallas import tpu as pltpu
from jax.sharding import PartitionSpec as P

F32 = jnp.float32
BF16 = jnp.bfloat16
MESH = pl.DeviceIdType.MESH

RIM = 16
COLS = 128
WIDE = COLS + 2 * RIM
OWN = 4
PAIR = 128

HALO_A, HALO_B, HALO_C = 5, 4, 2
REACH = 2

AROUND = tuple(
    (dr, dc) for dr in (-1, 1, 0, -2, 2) for dc in (0, -1, 1) if (dr, dc) != (0, 0)
)

EX_FIRST, EX_SECOND, EX_COT, EX_KERNELS = range(4)


def iota(shape, dim):
    return lax.broadcasted_iota(jnp.int32, shape, dim)


def one_hot(cond):
    return jnp.where(cond, 1.0, 0.0).astype(F32)


def low_lanes(shape):
    return iota(shape, len(shape) - 1) < 64


def kernel(
    rows,
    cols,
    feat,
    w_input,
    w_middle,
    w_output,
    w_merge,
    w_first,
    w_second,
    w_head,
    cot,
    up_out,
    adj_out,
    feat_v,
    w_input_v,
    w_middle_v,
    w_output_v,
    w_merge_v,
    w_first_v,
    w_second_v,
    w_head_v,
    cot_v,
    stage,
    xf1,
    xf2,
    xo2,
    cb,
    s1,
    s2,
    lift1,
    inner1,
    state1,
    lift2,
    inner2,
    lift3,
    inner3,
    merged,
    slope_m,
    rec_inner,
    refined,
    grad_ref,
    grad_in_pre,
    grad_in,
    grad_pre,
    k_feat,
    k_state,
    k_middle,
    k_output,
    k_feat_o,
    k_middle_o,
    k_output_o,
    k_merge2,
    k_merge1,
    k_first,
    k_second,
    k_head,
    k_head_t,
    k_second_t,
    k_first_t,
    k_merge_t,
    head_rows,
    shuffle,
    z_hi,
    z_lo,
    up_v,
    adj_v,
    col_mask,
    load_sem,
    store_sem,
    send_sem,
    recv_sem,
):
    sec = lax.axis_index("section")
    row = lax.axis_index("row")
    col = lax.axis_index("col")
    other = 1 - sec
    first_frame = 1 - sec
    second_frame = sec

    loads = []

    def load(source, target):
        copy = pltpu.make_async_copy(source, target, load_sem.at[len(loads)])
        copy.start()
        loads.append(copy)
        return copy

    load_f1 = load(feat.at[first_frame], feat_v.at[0])
    load_f2 = load(feat.at[second_frame], feat_v.at[1])
    load_cot = load(cot, cot_v)
    load_prop = [load(w_input, w_input_v), load(w_middle, w_middle_v), load(w_output, w_output_v)]
    load_head = load(w_head, w_head_v)
    load_second = load(w_second, w_second_v)
    load_merge = load(w_merge, w_merge_v)
    load_first = load(w_first, w_first_v)

    barrier = pltpu.get_barrier_semaphore()

    def exists(dr, dc):
        there = None
        for at, size, d in ((row, rows, dr), (col, cols, dc)):
            if d != 0:
                ok = at + d < size if d > 0 else at + d >= 0
                there = ok if there is None else there & ok
        return there

    def place(dr, dc):
        return (sec, lax.rem(row + dr + rows, rows), lax.rem(col + dc + cols, cols))

    for dr, dc in AROUND:

        @pl.when(exists(dr, dc))
        def _(dr=dr, dc=dc):
            pl.semaphore_signal(barrier, inc=1, device_id=place(dr, dc), device_id_type=MESH)

    @pl.when(sec == 1)
    def _():
        pl.semaphore_signal(barrier, inc=1, device_id=(other, row, col), device_id_type=MESH)

    near_rows = jnp.minimum(row + REACH, rows - 1) - jnp.maximum(row - REACH, 0) + 1
    near_cols = jnp.minimum(col + 1, cols - 1) - jnp.maximum(col - 1, 0) + 1
    greetings = near_rows * near_cols - sec

    def exchange(kind, buf, halo):
        copies = []
        for k, (dr, dc) in enumerate(AROUND):
            if abs(dr) == 2 and halo <= OWN:
                continue
            n = {0: OWN, 1: min(halo, OWN), 2: halo - OWN}[abs(dr)]
            sp = OWN - n if dr > 0 else 0
            dp = halo + sp - OWN * dr
            sc, m, dcol = {
                -1: (0, RIM, RIM + COLS),
                0: (0, COLS, RIM),
                1: (COLS - RIM, RIM, 0),
            }[dc]
            copy = pltpu.make_async_remote_copy(
                src_ref=buf.at[pl.ds(halo + sp, n), pl.ds(RIM + sc, m), :],
                dst_ref=buf.at[pl.ds(dp, n), pl.ds(dcol, m), :],
                send_sem=send_sem.at[kind, k],
                recv_sem=recv_sem.at[kind, k],
                device_id=place(dr, dc),
                device_id_type=MESH,
            )
            copies.append((copy, exists(dr, dc), exists(-dr, -dc)))
        return copies

    def start_all(copies):
        for copy, to, _ in copies:
            pl.when(to)(copy.start)

    def receive_all(copies):
        for copy, _, source in copies:
            pl.when(source)(copy.wait_recv)

    def sent_all(copies):
        for copy, to, _ in copies:
            pl.when(to)(copy.wait_send)

    halos = ((xf1, HALO_A), (xf2, HALO_B), (cb, HALO_C))

    def clear_rows(up, tiles):
        for buf, halo in halos:
            n = halo - OWN * tiles
            if n > 0:
                at = 0 if up else buf.shape[0] - n
                buf[pl.ds(at, n)] = jnp.zeros((n, WIDE, PAIR), BF16)

    def clear_cols(at):
        for buf, _ in halos:
            buf[:, pl.ds(at, RIM), :] = jnp.zeros((buf.shape[0], RIM, PAIR), BF16)

    for tiles in range(REACH):
        pl.when(row == tiles)(functools.partial(clear_rows, True, tiles))
        pl.when(row == rows - 1 - tiles)(functools.partial(clear_rows, False, tiles))
    pl.when(col == 0)(functools.partial(clear_cols, 0))
    pl.when(col == cols - 1)(functools.partial(clear_cols, RIM + COLS))

    def turn_features(at, dst, halo):
        stage[...] = feat_v[at].astype(F32)
        for p in range(OWN):
            two = jnp.concatenate(
                [stage[pl.ds(2 * p + r, 64, stride=8), :] for r in range(2)], axis=0
            )
            dst[halo + p, pl.ds(RIM, COLS), :] = two.T.astype(BF16)

    load_f1.wait()
    turn_features(0, xf1, HALO_A)
    pl.semaphore_wait(barrier, greetings)
    ex_first = exchange(EX_FIRST, xf1, HALO_A)
    start_all(ex_first)
    load_f2.wait()
    turn_features(1, xf2, HALO_B)
    ex_second = exchange(EX_SECOND, xf2, HALO_B)
    start_all(ex_second)

    k_at, n_at = iota((512, 512), 0), iota((512, 512), 1)
    shuffle[...] = one_hot(n_at == 4 * (k_at & 127) + (k_at >> 7)).astype(BF16)
    m_at, n_at = iota((128, 96), 0), iota((128, 96), 1)
    spread = one_hot(
        (((n_at >> 2) & 7) == (m_at >> 4)) & (((n_at >> 5) * 4 + (n_at & 3)) == (m_at & 15))
    ).astype(BF16)
    load_cot.wait()
    spaced = jnp.dot(spread, cot_v[...], preferred_element_type=F32).astype(BF16)
    parted = lax.dot_general(
        spaced, shuffle[...], (((1,), (1,)), ((), ())), preferred_element_type=F32
    )
    for p in range(OWN):
        pieces = [
            parted[(2 * p + r) * 16 : (2 * p + r + 1) * 16, j * 128 : (j + 1) * 128]
            for r in range(2)
            for j in range(4)
        ]
        cb[HALO_C + p, pl.ds(RIM, COLS), :] = jnp.concatenate(pieces, axis=0).T.astype(BF16)
    ex_cot = exchange(EX_COT, cb, HALO_C)
    start_all(ex_cot)

    col_at = iota((WIDE, PAIR), 0) - RIM + col * COLS
    col_mask[...] = one_hot((col_at >= 0) & (col_at < cols * COLS))

    def pack_forward(tap, targets):
        empty = jnp.zeros(tap(0, 0).shape, F32)
        for b in range(3):
            for q in range(4):
                upper = tap(q, b) if q < 3 else empty
                lower = tap(q - 1, b) if q > 0 else empty
                turned = jnp.concatenate([upper, lower], axis=0).T.astype(BF16)
                for t, target in enumerate(targets):
                    target[q * 64 : (q + 1) * 64, b * 128 : (b + 1) * 128] = turned[
                        t * 64 : (t + 1) * 64
                    ]

    def pack_transposed(tap, target):
        width = tap(0, 0).shape[1]
        empty = jnp.zeros((64, width), F32)
        for b in range(3):
            for q in range(4):
                left = tap(q, b) if q < 3 else empty
                right = tap(q - 1, b) if q > 0 else empty
                target[q * 64 : (q + 1) * 64, b * 2 * width : (b + 1) * 2 * width] = (
                    jnp.concatenate([left, right], axis=1).astype(BF16)
                )

    for copy in load_prop:
        copy.wait()
    pack_forward(lambda a, b: w_input_v[a, b].astype(F32), (k_feat, k_state))
    pack_forward(lambda a, b: w_middle_v[a, b].astype(F32), (k_middle,))
    pack_forward(lambda a, b: w_output_v[a, b].astype(F32), (k_output,))
    ex_kernels = [
        pltpu.make_async_remote_copy(
            src_ref=mine,
            dst_ref=theirs,
            send_sem=send_sem.at[EX_KERNELS, k],
            recv_sem=recv_sem.at[EX_KERNELS, k],
            device_id=(other, row, col),
            device_id_type=MESH,
        )
        for k, (mine, theirs) in enumerate(
            ((k_feat, k_feat_o), (k_middle, k_middle_o), (k_output, k_output_o))
        )
    ]

    @pl.when(sec == 0)
    def _():
        for copy in ex_kernels:
            copy.start()

    load_head.wait()
    m_at, n_at = iota((64, 48), 0), iota((64, 48), 1)
    order = one_hot((n_at == (m_at & 15) * 4 + (m_at >> 4)) & ((m_at & 15) < 12)).astype(BF16)
    for a in range(3):
        for b in range(3):
            head_rows[a, b] = jnp.dot(order, w_head_v[a, b], preferred_element_type=F32)
    pack_transposed(lambda a, b: head_rows[2 - a, 2 - b], k_head_t)
    load_second.wait()
    pack_transposed(lambda a, b: w_second_v[2 - a, 2 - b].astype(F32), k_second_t)

    load_merge.wait()

    @pl.when(sec == 0)
    def _():
        pack_forward(lambda a, b: w_merge_v[a, b].astype(F32), (k_merge2, k_merge1))

    @pl.when(sec == 1)
    def _():
        pack_forward(lambda a, b: w_merge_v[a, b].astype(F32), (k_merge1, k_merge2))

    load_first.wait()
    pack_forward(lambda a, b: w_first_v[a, b].astype(F32), (k_first,))
    pack_forward(lambda a, b: w_second_v[a, b].astype(F32), (k_second,))
    pack_forward(lambda a, b: head_rows[a, b], (k_head,))
    pack_transposed(lambda a, b: w_first_v[2 - a, 2 - b].astype(F32), k_first_t)
    pack_transposed(lambda a, b: w_merge_v[2 - a, 2 - b].astype(F32), k_merge_t)

    def conv(sources, matrices, j):
        total = None
        for source, matrix in zip(sources, matrices):
            x = jnp.concatenate([source[j], source[j + 1]], axis=1)
            y = jnp.dot(x, matrix[...], preferred_element_type=F32)
            total = y if total is None else total + y
        w = total.shape[1] // 3
        return (
            total[:, w : 2 * w]
            + pltpu.roll(total[:, :w], 1, 0)
            + pltpu.roll(total[:, 2 * w :], WIDE - 1, 0)
        )

    def inside(start):
        at = row * (2 * OWN) + start + jnp.where(low_lanes((1, PAIR)), 0, 1)
        return col_mask[...] * one_hot((at >= 0) & (at < rows * 2 * OWN))

    def lrelu(v):
        return jnp.where(v > 0, v, 0.1 * v)

    def realign(upper_of, lower_of):
        mixed = jnp.where(
            low_lanes(upper_of.shape), lower_of.astype(F32), upper_of.astype(F32)
        )
        return pltpu.roll(mixed, 64, 1).astype(BF16)

    receive_all(ex_first)
    for j in range(13):
        v = conv((xf1,), (k_feat,), j)
        lift1[j] = (lrelu(v) * inside(2 * j - 9)).astype(BF16)
    for j in range(12):
        v = conv((lift1,), (k_middle,), j)
        inner1[j] = (jnp.maximum(v, 0.0) * inside(2 * j - 8)).astype(BF16)
    for j in range(11):
        v = conv((inner1,), (k_output,), j) + lift1[j + 1].astype(F32)
        state1[j] = (v * inside(2 * j - 7)).astype(BF16)

    @pl.when(sec == 1)
    def _():
        for copy in ex_kernels:
            copy.wait_recv()
        for copy in ex_kernels:
            copy.start()

    receive_all(ex_second)
    for j in range(11):
        xo2[j] = realign(xf2[j], xf2[j + 1])
    for j in range(10):
        v = conv((xo2, state1), (k_feat, k_state), j)
        lift2[j] = (lrelu(v) * inside(2 * j - 6)).astype(BF16)
    for j in range(9):
        v = conv((lift2,), (k_middle,), j)
        inner2[j] = (jnp.maximum(v, 0.0) * inside(2 * j - 5)).astype(BF16)
    for j in range(8):
        v = conv((inner2,), (k_output,), j) + lift2[j + 1].astype(F32)
        s2[j] = (v * inside(2 * j - 4)).astype(BF16)

    receive_all(ex_cot)
    for j in range(7):
        v = conv((cb,), (k_head_t,), j)
        grad_ref[j] = (v * inside(2 * j - 3)).astype(BF16)
    for j in range(6):
        grad_in_pre[j] = conv((grad_ref,), (k_second_t,), j) * inside(2 * j - 2)

    @pl.when(sec == 0)
    def _():
        for copy in ex_kernels:
            copy.wait_recv()

    for j in range(10):
        v = conv((xo2,), (k_feat_o,), j)
        lift3[j] = (lrelu(v) * inside(2 * j - 6)).astype(BF16)
    for j in range(9):
        v = conv((lift3,), (k_middle_o,), j)
        inner3[j] = (jnp.maximum(v, 0.0) * inside(2 * j - 5)).astype(BF16)
    for j in range(8):
        v = conv((inner3,), (k_output_o,), j) + lift3[j + 1].astype(F32)
        s1[j] = (v * inside(2 * j - 4)).astype(BF16)

    for j in range(7):
        v = conv((s1, s2), (k_merge1, k_merge2), j)
        sigma = jax.nn.sigmoid(v)
        merged[j] = (v * sigma * inside(2 * j - 3)).astype(BF16)
        if 1 <= j <= 5:
            slope_m[j - 1] = sigma * (1.0 + v * (1.0 - sigma)) * inside(2 * j - 3)
    for j in range(6):
        v = conv((merged,), (k_first,), j)
        sigma = jax.nn.sigmoid(v)
        rec_inner[j] = (v * sigma * inside(2 * j - 2)).astype(BF16)
        grad_in[j] = (grad_in_pre[j] * (sigma * (1.0 + v * (1.0 - sigma)))).astype(BF16)
    for j in range(5):
        v = conv((rec_inner,), (k_second,), j) + merged[j + 1].astype(F32)
        refined[j] = (v * inside(2 * j - 1)).astype(BF16)
    for j in range(4):
        v = conv((refined,), (k_head,), j)[RIM : RIM + COLS].T
        high = v.astype(BF16)
        low = (v - high.astype(F32)).astype(BF16)
        for r in range(2):
            for i in range(4):
                piece = slice((r * 4 + i) * 16, (r * 4 + i + 1) * 16)
                at = (slice((2 * j + r) * 16, (2 * j + r + 1) * 16), slice(i * 128, (i + 1) * 128))
                z_hi[at] = high[piece]
                z_lo[at] = low[piece]
    m_at, n_at = iota((96, 128), 0), iota((96, 128), 1)
    gather = one_hot(
        (((m_at >> 2) & 7) == (n_at >> 4)) & (((m_at >> 5) * 4 + (m_at & 3)) == (n_at & 15))
    ).astype(BF16)
    total = None
    for z in (z_hi, z_lo):
        ordered = jnp.dot(gather, z[...], preferred_element_type=F32).astype(BF16)
        part = jnp.dot(ordered, shuffle[...], preferred_element_type=F32)
        total = part if total is None else total + part
    up_v[...] = total
    store_up = pltpu.make_async_copy(up_v, up_out, store_sem.at[0])
    store_up.start()

    for j in range(5):
        v = conv((grad_in,), (k_first_t,), j) + grad_ref[j + 1].astype(F32)
        grad_pre[j] = (v * slope_m[j]).astype(BF16)
    for j in range(4):
        v = conv((grad_pre,), (k_merge_t,), j)
        for r in range(2):
            adj_v[pl.ds(2 * j + r, 128, stride=8), :] = v[
                RIM : RIM + COLS, r * 128 : (r + 1) * 128
            ].T
    store_adj = pltpu.make_async_copy(adj_v, adj_out, store_sem.at[1])
    store_adj.start()

    for copies in (ex_first, ex_second, ex_cot):
        sent_all(copies)
    for copy in ex_kernels:
        copy.wait_send()
    store_up.wait()
    store_adj.wait()


def on_device(
    rows,
    cols,
    features,
    prop_input,
    prop_middle,
    prop_output,
    merge_weight,
    first_weight,
    second_weight,
    head_weight,
    cotangent,
):
    def taps(weight):
        return jnp.transpose(weight, (2, 3, 0, 1))

    def vmem(*shape, dtype=BF16):
        return pltpu.VMEM(shape, dtype)

    def act(pairs, dtype=BF16):
        return pltpu.VMEM((pairs, WIDE, PAIR), dtype)

    scratch = (
        [
            vmem(2, 512, 128),
            vmem(3, 3, 64, 128),
            vmem(3, 3, 64, 64),
            vmem(3, 3, 64, 64),
            vmem(3, 3, 64, 128),
            vmem(3, 3, 64, 64),
            vmem(3, 3, 64, 64),
            vmem(3, 3, 48, 64),
            vmem(96, 512),
            vmem(512, 128, dtype=F32),
            act(OWN + 2 * HALO_A),
            act(OWN + 2 * HALO_B),
            act(11),
            act(OWN + 2 * HALO_C),
            act(8),
            act(8),
            act(13),
            act(12),
            act(11),
            act(10),
            act(9),
            act(10),
            act(9),
            act(7),
            act(5, F32),
            act(6),
            act(5),
            act(7),
            act(6, F32),
            act(6),
            act(5),
        ]
        + [vmem(256, 384) for _ in range(15)]
        + [
            vmem(256, 768),
            vmem(3, 3, 64, 64, dtype=F32),
            vmem(512, 512),
            vmem(128, 512),
            vmem(128, 512),
            vmem(96, 512, dtype=F32),
            vmem(1024, 128, dtype=F32),
            vmem(WIDE, PAIR, dtype=F32),
            pltpu.SemaphoreType.DMA((10,)),
            pltpu.SemaphoreType.DMA((2,)),
            pltpu.SemaphoreType.DMA((4, len(AROUND))),
            pltpu.SemaphoreType.DMA((4, len(AROUND))),
        ]
    )
    up, adj = pl.pallas_call(
        functools.partial(kernel, rows, cols),
        out_shape=(
            jax.ShapeDtypeStruct((96, 512), F32),
            jax.ShapeDtypeStruct((1024, 128), F32),
        ),
        in_specs=[pl.BlockSpec(memory_space=pl.ANY)] * 9,
        out_specs=(pl.BlockSpec(memory_space=pl.ANY), pl.BlockSpec(memory_space=pl.ANY)),
        scratch_shapes=scratch,
        compiler_params=pltpu.CompilerParams(
            collective_id=0, has_side_effects=True, vmem_limit_bytes=60 * 1024 * 1024
        ),
    )(
        features.reshape(2, 512, 128),
        taps(prop_input[0]),
        taps(prop_middle[0]),
        taps(prop_output[0]),
        taps(merge_weight),
        taps(first_weight),
        taps(second_weight),
        taps(head_weight),
        cotangent.reshape(96, 512),
    )
    return up.reshape(1, 3, 32, 512), adj.reshape(1, 128, 8, 128)


def solution(mesh):
    rows, cols = mesh.shape["row"], mesh.shape["col"]
    placed = (
        P(None, None, "row", "col"),
        P("section", None, None, None, None),
        P("section", None, None, None, None),
        P("section", None, None, None, None),
        P(),
        P(),
        P(),
        P(),
        P("section", None, "row", "col"),
    )
    return jax.shard_map(
        functools.partial(on_device, rows, cols),
        mesh=mesh,
        in_specs=placed,
        out_specs=(P("section", None, "row", "col"), P("section", None, "row", "col")),
        check_vma=False,
    )
```

```python
import functools

import jax
import jax.numpy as jnp
from jax import lax
from jax.experimental import pallas as pl
from jax.experimental.pallas import tpu as pltpu
from jax.sharding import PartitionSpec as P

F32 = jnp.float32
BF16 = jnp.bfloat16
MESH = pl.DeviceIdType.MESH

RIM = 16
COLS = 128
WIDE = COLS + 2 * RIM
OWN = 4
PAIR = 128

HALO_A, HALO_B, HALO_C = 5, 4, 2
REACH = 2

AROUND = tuple(
    (dr, dc) for dr in (-1, 1, 0, -2, 2) for dc in (0, -1, 1) if (dr, dc) != (0, 0)
)

EX_FIRST, EX_SECOND, EX_COT, EX_STATE = range(4)


def iota(shape, dim):
    return lax.broadcasted_iota(jnp.int32, shape, dim)


def one_hot(cond):
    return jnp.where(cond, 1.0, 0.0).astype(F32)


def low_lanes(shape):
    return iota(shape, len(shape) - 1) < 64


def kernel(
    rows,
    cols,
    feat,
    w_input,
    w_middle,
    w_output,
    w_merge,
    w_first,
    w_second,
    w_head,
    cot,
    up_out,
    adj_out,
    feat_v,
    w_input_v,
    w_middle_v,
    w_output_v,
    w_merge_v,
    w_first_v,
    w_second_v,
    w_head_v,
    cot_v,
    stage,
    xf1,
    xf2,
    xo2,
    cb,
    s1,
    s2,
    lift1,
    inner1,
    state1,
    lift2,
    inner2,
    e1,
    merged,
    slope_m,
    rec_inner,
    refined,
    grad_ref,
    grad_in_pre,
    grad_in,
    grad_pre,
    k_feat,
    k_state,
    k_middle,
    k_output,
    k_merge2,
    k_merge1,
    k_first,
    k_second,
    k_head,
    k_head_t,
    k_second_t,
    k_first_t,
    k_merge_t,
    head_rows,
    shuffle,
    z_hi,
    z_lo,
    up_v,
    adj_v,
    col_mask,
    load_sem,
    store_sem,
    send_sem,
    recv_sem,
):
    sec = lax.axis_index("section")
    row = lax.axis_index("row")
    col = lax.axis_index("col")
    other = 1 - sec
    first_frame = 1 - sec
    second_frame = sec

    loads = []

    def load(source, target):
        copy = pltpu.make_async_copy(source, target, load_sem.at[len(loads)])
        copy.start()
        loads.append(copy)
        return copy

    load_f1 = load(feat.at[first_frame], feat_v.at[0])
    load_f2 = load(feat.at[second_frame], feat_v.at[1])
    load_cot = load(cot, cot_v)
    load_prop = [load(w_input, w_input_v), load(w_middle, w_middle_v), load(w_output, w_output_v)]
    load_head = load(w_head, w_head_v)
    load_second = load(w_second, w_second_v)
    load_merge = load(w_merge, w_merge_v)
    load_first = load(w_first, w_first_v)

    barrier = pltpu.get_barrier_semaphore()

    def exists(dr, dc):
        there = None
        for at, size, d in ((row, rows, dr), (col, cols, dc)):
            if d != 0:
                ok = at + d < size if d > 0 else at + d >= 0
                there = ok if there is None else there & ok
        return there

    def place(dr, dc):
        return (sec, lax.rem(row + dr + rows, rows), lax.rem(col + dc + cols, cols))

    for dr, dc in AROUND:

        @pl.when(exists(dr, dc))
        def _(dr=dr, dc=dc):
            pl.semaphore_signal(barrier, inc=1, device_id=place(dr, dc), device_id_type=MESH)

    pl.semaphore_signal(barrier, inc=1, device_id=(other, row, col), device_id_type=MESH)
    near_rows = jnp.minimum(row + REACH, rows - 1) - jnp.maximum(row - REACH, 0) + 1
    near_cols = jnp.minimum(col + 1, cols - 1) - jnp.maximum(col - 1, 0) + 1
    greetings = near_rows * near_cols

    def exchange(kind, buf, halo):
        copies = []
        for k, (dr, dc) in enumerate(AROUND):
            if abs(dr) == 2 and halo <= OWN:
                continue
            n = {0: OWN, 1: min(halo, OWN), 2: halo - OWN}[abs(dr)]
            sp = OWN - n if dr > 0 else 0
            dp = halo + sp - OWN * dr
            sc, m, dcol = {
                -1: (0, RIM, RIM + COLS),
                0: (0, COLS, RIM),
                1: (COLS - RIM, RIM, 0),
            }[dc]
            copy = pltpu.make_async_remote_copy(
                src_ref=buf.at[pl.ds(halo + sp, n), pl.ds(RIM + sc, m), :],
                dst_ref=buf.at[pl.ds(dp, n), pl.ds(dcol, m), :],
                send_sem=send_sem.at[kind, k],
                recv_sem=recv_sem.at[kind, k],
                device_id=place(dr, dc),
                device_id_type=MESH,
            )
            copies.append((copy, exists(dr, dc), exists(-dr, -dc)))
        return copies

    def start_all(copies):
        for copy, to, _ in copies:
            pl.when(to)(copy.start)

    def receive_all(copies):
        for copy, _, source in copies:
            pl.when(source)(copy.wait_recv)

    def sent_all(copies):
        for copy, to, _ in copies:
            pl.when(to)(copy.wait_send)

    halos = ((xf1, HALO_A), (cb, HALO_C))

    def clear_rows(up, tiles):
        for buf, halo in halos:
            n = halo - OWN * tiles
            if n > 0:
                at = 0 if up else buf.shape[0] - n
                buf[pl.ds(at, n)] = jnp.zeros((n, WIDE, PAIR), BF16)

    def clear_cols(at):
        for buf, _ in halos:
            buf[:, pl.ds(at, RIM), :] = jnp.zeros((buf.shape[0], RIM, PAIR), BF16)

    for tiles in range(REACH):
        pl.when(row == tiles)(functools.partial(clear_rows, True, tiles))
        pl.when(row == rows - 1 - tiles)(functools.partial(clear_rows, False, tiles))
    pl.when(col == 0)(functools.partial(clear_cols, 0))
    pl.when(col == cols - 1)(functools.partial(clear_cols, RIM + COLS))

    def turn_features(at, dst, halo):
        stage[...] = feat_v[at].astype(F32)
        for p in range(OWN):
            two = jnp.concatenate(
                [stage[pl.ds(2 * p + r, 64, stride=8), :] for r in range(2)], axis=0
            )
            dst[halo + p, pl.ds(RIM, COLS), :] = two.T.astype(BF16)

    load_f1.wait()
    turn_features(0, xf1, HALO_A)
    pl.semaphore_wait(barrier, greetings)
    ex_first = exchange(EX_FIRST, xf1, HALO_A)
    start_all(ex_first)
    load_f2.wait()
    turn_features(1, xf2, HALO_B)

    def pass_on(kind, parts):
        return [
            pltpu.make_async_remote_copy(
                src_ref=src,
                dst_ref=dst,
                send_sem=send_sem.at[kind, k],
                recv_sem=recv_sem.at[kind, k],
                device_id=(other, row, col),
                device_id_type=MESH,
            )
            for k, (src, dst) in enumerate(parts)
        ]

    def same(at, n, start, width):
        return tuple(
            buf.at[pl.ds(halo + at, n), pl.ds(start, width), :]
            for buf, halo in ((xf1, HALO_A), (xf2, HALO_B))
        )

    ex_second = pass_on(
        EX_SECOND,
        (
            same(-HALO_B, HALO_B, 0, WIDE),
            same(OWN, HALO_B, 0, WIDE),
            same(0, OWN, 0, RIM),
            same(0, OWN, RIM + COLS, RIM),
        ),
    )
    ex_state = pass_on(EX_STATE, ((e1, s1),))

    k_at, n_at = iota((512, 512), 0), iota((512, 512), 1)
    shuffle[...] = one_hot(n_at == 4 * (k_at & 127) + (k_at >> 7)).astype(BF16)
    m_at, n_at = iota((128, 96), 0), iota((128, 96), 1)
    spread = one_hot(
        (((n_at >> 2) & 7) == (m_at >> 4)) & (((n_at >> 5) * 4 + (n_at & 3)) == (m_at & 15))
    ).astype(BF16)
    load_cot.wait()
    spaced = jnp.dot(spread, cot_v[...], preferred_element_type=F32).astype(BF16)
    parted = lax.dot_general(
        spaced, shuffle[...], (((1,), (1,)), ((), ())), preferred_element_type=F32
    )
    for p in range(OWN):
        pieces = [
            parted[(2 * p + r) * 16 : (2 * p + r + 1) * 16, j * 128 : (j + 1) * 128]
            for r in range(2)
            for j in range(4)
        ]
        cb[HALO_C + p, pl.ds(RIM, COLS), :] = jnp.concatenate(pieces, axis=0).T.astype(BF16)
    ex_cot = exchange(EX_COT, cb, HALO_C)
    start_all(ex_cot)

    col_at = iota((WIDE, PAIR), 0) - RIM + col * COLS
    col_mask[...] = one_hot((col_at >= 0) & (col_at < cols * COLS))

    def pack_forward(tap, targets):
        empty = jnp.zeros(tap(0, 0).shape, F32)
        for b in range(3):
            for q in range(4):
                upper = tap(q, b) if q < 3 else empty
                lower = tap(q - 1, b) if q > 0 else empty
                turned = jnp.concatenate([upper, lower], axis=0).T.astype(BF16)
                for t, target in enumerate(targets):
                    target[q * 64 : (q + 1) * 64, b * 128 : (b + 1) * 128] = turned[
                        t * 64 : (t + 1) * 64
                    ]

    def pack_transposed(tap, target):
        width = tap(0, 0).shape[1]
        empty = jnp.zeros((64, width), F32)
        for b in range(3):
            for q in range(4):
                left = tap(q, b) if q < 3 else empty
                right = tap(q - 1, b) if q > 0 else empty
                target[q * 64 : (q + 1) * 64, b * 2 * width : (b + 1) * 2 * width] = (
                    jnp.concatenate([left, right], axis=1).astype(BF16)
                )

    for copy in load_prop:
        copy.wait()
    pack_forward(lambda a, b: w_input_v[a, b].astype(F32), (k_feat, k_state))
    pack_forward(lambda a, b: w_middle_v[a, b].astype(F32), (k_middle,))
    pack_forward(lambda a, b: w_output_v[a, b].astype(F32), (k_output,))

    load_head.wait()
    m_at, n_at = iota((64, 48), 0), iota((64, 48), 1)
    order = one_hot((n_at == (m_at & 15) * 4 + (m_at >> 4)) & ((m_at & 15) < 12)).astype(BF16)
    for a in range(3):
        for b in range(3):
            head_rows[a, b] = jnp.dot(order, w_head_v[a, b], preferred_element_type=F32)
    pack_transposed(lambda a, b: head_rows[2 - a, 2 - b], k_head_t)
    load_second.wait()
    pack_transposed(lambda a, b: w_second_v[2 - a, 2 - b].astype(F32), k_second_t)

    load_merge.wait()

    @pl.when(sec == 0)
    def _():
        pack_forward(lambda a, b: w_merge_v[a, b].astype(F32), (k_merge2, k_merge1))

    @pl.when(sec == 1)
    def _():
        pack_forward(lambda a, b: w_merge_v[a, b].astype(F32), (k_merge1, k_merge2))

    load_first.wait()
    pack_forward(lambda a, b: w_first_v[a, b].astype(F32), (k_first,))
    pack_forward(lambda a, b: w_second_v[a, b].astype(F32), (k_second,))
    pack_forward(lambda a, b: head_rows[a, b], (k_head,))
    pack_transposed(lambda a, b: w_first_v[2 - a, 2 - b].astype(F32), k_first_t)
    pack_transposed(lambda a, b: w_merge_v[2 - a, 2 - b].astype(F32), k_merge_t)

    def conv(sources, matrices, j):
        total = None
        for source, matrix in zip(sources, matrices):
            x = jnp.concatenate([source[j], source[j + 1]], axis=1)
            y = jnp.dot(x, matrix[...], preferred_element_type=F32)
            total = y if total is None else total + y
        w = total.shape[1] // 3
        return (
            total[:, w : 2 * w]
            + pltpu.roll(total[:, :w], 1, 0)
            + pltpu.roll(total[:, 2 * w :], WIDE - 1, 0)
        )

    def inside(start):
        at = row * (2 * OWN) + start + jnp.where(low_lanes((1, PAIR)), 0, 1)
        return col_mask[...] * one_hot((at >= 0) & (at < rows * 2 * OWN))

    def lrelu(v):
        return jnp.where(v > 0, v, 0.1 * v)

    def realign(upper_of, lower_of):
        mixed = jnp.where(
            low_lanes(upper_of.shape), lower_of.astype(F32), upper_of.astype(F32)
        )
        return pltpu.roll(mixed, 64, 1).astype(BF16)

    receive_all(ex_first)
    for copy in ex_second:
        copy.start()
    for j in range(13):
        v = conv((xf1,), (k_feat,), j)
        lift1[j] = (lrelu(v) * inside(2 * j - 9)).astype(BF16)
    for j in range(12):
        v = conv((lift1,), (k_middle,), j)
        inner1[j] = (jnp.maximum(v, 0.0) * inside(2 * j - 8)).astype(BF16)
    for j in range(11):
        v = conv((inner1,), (k_output,), j) + lift1[j + 1].astype(F32)
        state1[j] = (v * inside(2 * j - 7)).astype(BF16)

    for m in range(8):
        e1[m] = realign(state1[m + 1], state1[m + 2])
    for copy in ex_state:
        copy.start()

    for copy in ex_second:
        copy.wait_recv()
    for j in range(11):
        xo2[j] = realign(xf2[j], xf2[j + 1])
    for j in range(10):
        v = conv((xo2, state1), (k_feat, k_state), j)
        lift2[j] = (lrelu(v) * inside(2 * j - 6)).astype(BF16)
    for j in range(9):
        v = conv((lift2,), (k_middle,), j)
        inner2[j] = (jnp.maximum(v, 0.0) * inside(2 * j - 5)).astype(BF16)
    for j in range(8):
        v = conv((inner2,), (k_output,), j) + lift2[j + 1].astype(F32)
        s2[j] = (v * inside(2 * j - 4)).astype(BF16)

    receive_all(ex_cot)
    for j in range(7):
        v = conv((cb,), (k_head_t,), j)
        grad_ref[j] = (v * inside(2 * j - 3)).astype(BF16)
    for j in range(6):
        grad_in_pre[j] = conv((grad_ref,), (k_second_t,), j) * inside(2 * j - 2)

    for copy in ex_state:
        copy.wait_recv()
    for j in range(7):
        v = conv((s1, s2), (k_merge1, k_merge2), j)
        sigma = jax.nn.sigmoid(v)
        merged[j] = (v * sigma * inside(2 * j - 3)).astype(BF16)
        if 1 <= j <= 5:
            slope_m[j - 1] = sigma * (1.0 + v * (1.0 - sigma)) * inside(2 * j - 3)
    for j in range(6):
        v = conv((merged,), (k_first,), j)
        sigma = jax.nn.sigmoid(v)
        rec_inner[j] = (v * sigma * inside(2 * j - 2)).astype(BF16)
        grad_in[j] = (grad_in_pre[j] * (sigma * (1.0 + v * (1.0 - sigma)))).astype(BF16)
    for j in range(5):
        v = conv((rec_inner,), (k_second,), j) + merged[j + 1].astype(F32)
        refined[j] = (v * inside(2 * j - 1)).astype(BF16)
    for j in range(4):
        v = conv((refined,), (k_head,), j)[RIM : RIM + COLS].T
        high = v.astype(BF16)
        low = (v - high.astype(F32)).astype(BF16)
        for r in range(2):
            for i in range(4):
                piece = slice((r * 4 + i) * 16, (r * 4 + i + 1) * 16)
                at = (slice((2 * j + r) * 16, (2 * j + r + 1) * 16), slice(i * 128, (i + 1) * 128))
                z_hi[at] = high[piece]
                z_lo[at] = low[piece]
    m_at, n_at = iota((96, 128), 0), iota((96, 128), 1)
    gather = one_hot(
        (((m_at >> 2) & 7) == (n_at >> 4)) & (((m_at >> 5) * 4 + (m_at & 3)) == (n_at & 15))
    ).astype(BF16)
    total = None
    for z in (z_hi, z_lo):
        ordered = jnp.dot(gather, z[...], preferred_element_type=F32).astype(BF16)
        part = jnp.dot(ordered, shuffle[...], preferred_element_type=F32)
        total = part if total is None else total + part
    up_v[...] = total
    store_up = pltpu.make_async_copy(up_v, up_out, store_sem.at[0])
    store_up.start()

    for j in range(5):
        v = conv((grad_in,), (k_first_t,), j) + grad_ref[j + 1].astype(F32)
        grad_pre[j] = (v * slope_m[j]).astype(BF16)
    for j in range(4):
        v = conv((grad_pre,), (k_merge_t,), j)
        for r in range(2):
            adj_v[pl.ds(2 * j + r, 128, stride=8), :] = v[
                RIM : RIM + COLS, r * 128 : (r + 1) * 128
            ].T
    store_adj = pltpu.make_async_copy(adj_v, adj_out, store_sem.at[1])
    store_adj.start()

    for copies in (ex_first, ex_cot):
        sent_all(copies)
    for copy in ex_second + ex_state:
        copy.wait_send()
    store_up.wait()
    store_adj.wait()


def hand_over(up_in, adj_in, up_out, adj_out, sem):
    copies = [pltpu.make_async_copy(up_in, up_out, sem.at[0])]
    for k in range(4):
        part = pl.ds(k * 256, 256)
        copies.append(pltpu.make_async_copy(adj_in.at[part], adj_out.at[part], sem.at[1 + k]))
    for copy in copies:
        copy.start()
    for copy in copies:
        copy.wait()


def on_device(
    rows,
    cols,
    features,
    prop_input,
    prop_middle,
    prop_output,
    merge_weight,
    first_weight,
    second_weight,
    head_weight,
    cotangent,
):
    def taps(weight):
        return jnp.transpose(weight, (2, 3, 0, 1))

    def vmem(*shape, dtype=BF16):
        return pltpu.VMEM(shape, dtype)

    def act(pairs, dtype=BF16):
        return pltpu.VMEM((pairs, WIDE, PAIR), dtype)

    scratch = (
        [
            vmem(2, 512, 128),
            vmem(3, 3, 64, 128),
            vmem(3, 3, 64, 64),
            vmem(3, 3, 64, 64),
            vmem(3, 3, 64, 128),
            vmem(3, 3, 64, 64),
            vmem(3, 3, 64, 64),
            vmem(3, 3, 48, 64),
            vmem(96, 512),
            vmem(512, 128, dtype=F32),
            act(OWN + 2 * HALO_A),
            act(OWN + 2 * HALO_B),
            act(11),
            act(OWN + 2 * HALO_C),
            act(8),
            act(8),
            act(13),
            act(12),
            act(11),
            act(10),
            act(9),
            act(8),
            act(7),
            act(5, F32),
            act(6),
            act(5),
            act(7),
            act(6, F32),
            act(6),
            act(5),
        ]
        + [vmem(256, 384) for _ in range(12)]
        + [
            vmem(256, 768),
            vmem(3, 3, 64, 64, dtype=F32),
            vmem(512, 512),
            vmem(128, 512),
            vmem(128, 512),
            vmem(96, 512, dtype=F32),
            vmem(1024, 128, dtype=F32),
            vmem(WIDE, PAIR, dtype=F32),
            pltpu.SemaphoreType.DMA((10,)),
            pltpu.SemaphoreType.DMA((2,)),
            pltpu.SemaphoreType.DMA((4, len(AROUND))),
            pltpu.SemaphoreType.DMA((4, len(AROUND))),
        ]
    )
    up, adj = pl.pallas_call(
        functools.partial(kernel, rows, cols),
        out_shape=(
            jax.ShapeDtypeStruct((96, 512), F32),
            jax.ShapeDtypeStruct((1024, 128), F32),
        ),
        in_specs=[pl.BlockSpec(memory_space=pl.ANY)] * 9,
        out_specs=(pl.BlockSpec(memory_space=pl.ANY), pl.BlockSpec(memory_space=pl.ANY)),
        scratch_shapes=scratch,
        compiler_params=pltpu.CompilerParams(
            collective_id=0, has_side_effects=True, vmem_limit_bytes=60 * 1024 * 1024
        ),
    )(
        features.reshape(2, 512, 128),
        taps(prop_input[0]),
        taps(prop_middle[0]),
        taps(prop_output[0]),
        taps(merge_weight),
        taps(first_weight),
        taps(second_weight),
        taps(head_weight),
        cotangent.reshape(96, 512),
    )
    up, adj = pl.pallas_call(
        hand_over,
        out_shape=(
            jax.ShapeDtypeStruct((96, 512), F32),
            jax.ShapeDtypeStruct((1024, 128), F32),
        ),
        in_specs=[pl.BlockSpec(memory_space=pl.ANY)] * 2,
        out_specs=(pl.BlockSpec(memory_space=pl.ANY), pl.BlockSpec(memory_space=pl.ANY)),
        scratch_shapes=[pltpu.SemaphoreType.DMA((5,))],
    )(up, adj)
    return up.reshape(1, 3, 32, 512), adj.reshape(1, 128, 8, 128)


def solution(mesh):
    rows, cols = mesh.shape["row"], mesh.shape["col"]
    placed = (
        P(None, None, "row", "col"),
        P("section", None, None, None, None),
        P("section", None, None, None, None),
        P("section", None, None, None, None),
        P(),
        P(),
        P(),
        P(),
        P("section", None, "row", "col"),
    )
    return jax.shard_map(
        functools.partial(on_device, rows, cols),
        mesh=mesh,
        in_specs=placed,
        out_specs=(P("section", None, "row", "col"), P("section", None, "row", "col")),
        check_vma=False,
    )
```

```python
import functools

import jax
import jax.numpy as jnp
from jax import lax
from jax.experimental import pallas as pl
from jax.experimental.pallas import tpu as pltpu
from jax.sharding import PartitionSpec as P

F32 = jnp.float32
BF16 = jnp.bfloat16
MESH = pl.DeviceIdType.MESH

RIM = 16
COLS = 128
WIDE = COLS + 2 * RIM
OWN = 4
PAIR = 128

HALO_A, HALO_B, HALO_C = 5, 4, 2
REACH = 2

AROUND = tuple(
    (dr, dc)
    for dc in (0, -1, 1)
    for dr in (-1, 1, 0, -2, 2)
    if (dr, dc) != (0, 0)
)

EX_FIRST, EX_SECOND, EX_COT, EX_STATE = range(4)


def iota(shape, dim):
    return lax.broadcasted_iota(jnp.int32, shape, dim)


def one_hot(cond):
    return jnp.where(cond, 1.0, 0.0).astype(F32)


def low_lanes(shape):
    return iota(shape, len(shape) - 1) < 64


def kernel(
    rows,
    cols,
    feat,
    w_input,
    w_middle,
    w_output,
    w_merge,
    w_first,
    w_second,
    w_head,
    cot,
    up_out,
    adj_out,
    feat_v,
    w_input_v,
    w_middle_v,
    w_output_v,
    w_merge_v,
    w_first_v,
    w_second_v,
    w_head_v,
    cot_v,
    stage,
    xf1,
    xf2,
    xo2,
    cb,
    s1,
    s2,
    lift1,
    inner1,
    state1,
    lift2,
    inner2,
    e1,
    merged,
    slope_m,
    rec_inner,
    refined,
    grad_ref,
    grad_in_pre,
    grad_in,
    grad_pre,
    k_prop,
    k_middle,
    k_output,
    k_merge,
    k_first,
    k_second,
    k_head,
    k_head_t,
    k_second_t,
    k_first_t,
    k_merge_t,
    head_rows,
    shuffle,
    z_hi,
    z_lo,
    col_mask,
    load_sem,
    send_sem,
    recv_sem,
):
    sec = lax.axis_index("section")
    row = lax.axis_index("row")
    col = lax.axis_index("col")
    other = 1 - sec
    first_frame = 1 - sec
    second_frame = sec

    loads = []

    def load(source, target):
        copy = pltpu.make_async_copy(source, target, load_sem.at[len(loads)])
        copy.start()
        loads.append(copy)
        return copy

    load_f1 = load(feat.at[first_frame], feat_v.at[0])

    barrier = pltpu.get_barrier_semaphore()

    def exists(dr, dc):
        there = None
        for at, size, d in ((row, rows, dr), (col, cols, dc)):
            if d != 0:
                ok = at + d < size if d > 0 else at + d >= 0
                there = ok if there is None else there & ok
        return there

    def place(dr, dc):
        return (sec, lax.rem(row + dr + rows, rows), lax.rem(col + dc + cols, cols))

    for dr, dc in AROUND:

        @pl.when(exists(dr, dc))
        def _(dr=dr, dc=dc):
            pl.semaphore_signal(barrier, inc=1, device_id=place(dr, dc), device_id_type=MESH)

    pl.semaphore_signal(barrier, inc=1, device_id=(other, row, col), device_id_type=MESH)
    load_f2 = load(feat.at[second_frame], feat_v.at[1])
    load_cot = load(cot, cot_v)
    load_prop = [load(w_input, w_input_v), load(w_middle, w_middle_v), load(w_output, w_output_v)]
    load_head = load(w_head, w_head_v)
    load_second = load(w_second, w_second_v)
    load_merge = load(w_merge, w_merge_v)
    load_first = load(w_first, w_first_v)

    near_rows = jnp.minimum(row + REACH, rows - 1) - jnp.maximum(row - REACH, 0) + 1
    near_cols = jnp.minimum(col + 1, cols - 1) - jnp.maximum(col - 1, 0) + 1
    greetings = near_rows * near_cols

    def exchange(kind, buf, halo):
        copies = []
        for k, (dr, dc) in enumerate(AROUND):
            if abs(dr) == 2 and halo <= OWN:
                continue
            n = {0: OWN, 1: min(halo, OWN), 2: halo - OWN}[abs(dr)]
            sp = OWN - n if dr > 0 else 0
            dp = halo + sp - OWN * dr
            sc, m, dcol = {
                -1: (0, RIM, RIM + COLS),
                0: (0, COLS, RIM),
                1: (COLS - RIM, RIM, 0),
            }[dc]
            copy = pltpu.make_async_remote_copy(
                src_ref=buf.at[pl.ds(halo + sp, n), pl.ds(RIM + sc, m), :],
                dst_ref=buf.at[pl.ds(dp, n), pl.ds(dcol, m), :],
                send_sem=send_sem.at[kind, k],
                recv_sem=recv_sem.at[kind, k],
                device_id=place(dr, dc),
                device_id_type=MESH,
            )
            copies.append((copy, exists(dr, dc), exists(-dr, -dc), dr))
        return copies

    def start_all(copies):
        for copy, to, _, _ in copies:
            pl.when(to)(copy.start)

    def receive_all(copies, tiles=(0, 1, 2)):
        for copy, _, source, dr in copies:
            if abs(dr) in tiles:
                pl.when(source)(copy.wait_recv)

    def sent_all(copies):
        for copy, to, _, _ in copies:
            pl.when(to)(copy.wait_send)

    halos = ((xf1, HALO_A), (cb, HALO_C))

    def clear_rows(up, tiles):
        for buf, halo in halos:
            n = halo - OWN * tiles
            if n > 0:
                at = 0 if up else buf.shape[0] - n
                buf[pl.ds(at, n)] = jnp.zeros((n, WIDE, PAIR), BF16)

    def clear_cols(at):
        for buf, _ in halos:
            buf[:, pl.ds(at, RIM), :] = jnp.zeros((buf.shape[0], RIM, PAIR), BF16)

    for tiles in range(REACH):
        pl.when(row == tiles)(functools.partial(clear_rows, True, tiles))
        pl.when(row == rows - 1 - tiles)(functools.partial(clear_rows, False, tiles))
    pl.when(col == 0)(functools.partial(clear_cols, 0))
    pl.when(col == cols - 1)(functools.partial(clear_cols, RIM + COLS))

    def turn_features(at, dst, halo):
        stage[...] = feat_v[at].astype(F32)
        for p in range(OWN):
            two = jnp.concatenate(
                [stage[pl.ds(2 * p + r, 64, stride=8), :] for r in range(2)], axis=0
            )
            dst[halo + p, pl.ds(RIM, COLS), :] = two.T.astype(BF16)

    load_f1.wait()
    turn_features(0, xf1, HALO_A)
    pl.semaphore_wait(barrier, greetings)
    ex_first = exchange(EX_FIRST, xf1, HALO_A)
    start_all(ex_first)
    load_f2.wait()
    turn_features(1, xf2, HALO_B)

    def pass_on(kind, parts):
        return [
            pltpu.make_async_remote_copy(
                src_ref=src,
                dst_ref=dst,
                send_sem=send_sem.at[kind, k],
                recv_sem=recv_sem.at[kind, k],
                device_id=(other, row, col),
                device_id_type=MESH,
            )
            for k, (src, dst) in enumerate(parts)
        ]

    def same(at, n, start, width):
        return tuple(
            buf.at[pl.ds(halo + at, n), pl.ds(start, width), :]
            for buf, halo in ((xf1, HALO_A), (xf2, HALO_B))
        )

    ex_second = pass_on(
        EX_SECOND,
        (
            same(-HALO_B, HALO_B, 0, WIDE),
            same(OWN, HALO_B, 0, WIDE),
            same(0, OWN, 0, RIM),
            same(0, OWN, RIM + COLS, RIM),
        ),
    )
    ex_state = pass_on(EX_STATE, ((e1, s1),))

    k_at, n_at = iota((512, 512), 0), iota((512, 512), 1)
    shuffle[...] = one_hot(n_at == 4 * (k_at & 127) + (k_at >> 7)).astype(BF16)
    m_at, n_at = iota((128, 96), 0), iota((128, 96), 1)
    spread = one_hot(
        (((n_at >> 2) & 7) == (m_at >> 4)) & (((n_at >> 5) * 4 + (n_at & 3)) == (m_at & 15))
    ).astype(BF16)
    load_cot.wait()
    spaced = jnp.dot(spread, cot_v[...], preferred_element_type=F32).astype(BF16)
    parted = lax.dot_general(
        spaced, shuffle[...], (((1,), (1,)), ((), ())), preferred_element_type=F32
    )
    for p in range(OWN):
        pieces = [
            parted[(2 * p + r) * 16 : (2 * p + r + 1) * 16, j * 128 : (j + 1) * 128]
            for r in range(2)
            for j in range(4)
        ]
        cb[HALO_C + p, pl.ds(RIM, COLS), :] = jnp.concatenate(pieces, axis=0).T.astype(BF16)
    ex_cot = exchange(EX_COT, cb, HALO_C)
    start_all(ex_cot)

    col_at = iota((WIDE, PAIR), 0) - RIM + col * COLS
    col_mask[...] = one_hot((col_at >= 0) & (col_at < cols * COLS))

    def pack_forward(tap, targets):
        empty = jnp.zeros(tap(0, 0).shape, F32)
        for b in range(3):
            for q in range(4):
                upper = tap(q, b) if q < 3 else empty
                lower = tap(q - 1, b) if q > 0 else empty
                turned = jnp.concatenate([upper, lower], axis=0).T.astype(BF16)
                for t, target in enumerate(targets):
                    target[q * 64 : (q + 1) * 64, b * 128 : (b + 1) * 128] = turned[
                        t * 64 : (t + 1) * 64
                    ]

    def pack_transposed(tap, target):
        width = tap(0, 0).shape[1]
        empty = jnp.zeros((64, width), F32)
        for b in range(3):
            for q in range(4):
                left = tap(q, b) if q < 3 else empty
                right = tap(q - 1, b) if q > 0 else empty
                target[q * 64 : (q + 1) * 64, b * 2 * width : (b + 1) * 2 * width] = (
                    jnp.concatenate([left, right], axis=1).astype(BF16)
                )

    for copy in load_prop:
        copy.wait()
    pack_forward(lambda a, b: w_input_v[a, b].astype(F32), (k_prop.at[pl.ds(0, 256)], k_prop.at[pl.ds(256, 256)]))
    pack_forward(lambda a, b: w_middle_v[a, b].astype(F32), (k_middle,))
    pack_forward(lambda a, b: w_output_v[a, b].astype(F32), (k_output,))

    load_head.wait()
    m_at, n_at = iota((64, 48), 0), iota((64, 48), 1)
    order = one_hot((n_at == (m_at & 15) * 4 + (m_at >> 4)) & ((m_at & 15) < 12)).astype(BF16)
    for a in range(3):
        for b in range(3):
            head_rows[a, b] = jnp.dot(order, w_head_v[a, b], preferred_element_type=F32)
    pack_transposed(lambda a, b: head_rows[2 - a, 2 - b], k_head_t)
    load_second.wait()
    pack_transposed(lambda a, b: w_second_v[2 - a, 2 - b].astype(F32), k_second_t)

    load_merge.wait()

    @pl.when(sec == 0)
    def _():
        pack_forward(lambda a, b: w_merge_v[a, b].astype(F32), (k_merge.at[pl.ds(256, 256)], k_merge.at[pl.ds(0, 256)]))

    @pl.when(sec == 1)
    def _():
        pack_forward(lambda a, b: w_merge_v[a, b].astype(F32), (k_merge.at[pl.ds(0, 256)], k_merge.at[pl.ds(256, 256)]))

    load_first.wait()
    pack_forward(lambda a, b: w_first_v[a, b].astype(F32), (k_first,))
    pack_forward(lambda a, b: w_second_v[a, b].astype(F32), (k_second,))
    pack_forward(lambda a, b: head_rows[a, b], (k_head,))
    pack_transposed(lambda a, b: w_first_v[2 - a, 2 - b].astype(F32), k_first_t)
    pack_transposed(lambda a, b: w_merge_v[2 - a, 2 - b].astype(F32), k_merge_t)

    def conv(sources, matrix, j):
        x = jnp.concatenate([s[j + k] for s in sources for k in range(2)], axis=1)
        total = jnp.dot(x, matrix[...], preferred_element_type=F32)
        w = total.shape[1] // 3
        return (
            total[:, w : 2 * w]
            + pltpu.roll(total[:, :w], 1, 0)
            + pltpu.roll(total[:, 2 * w :], WIDE - 1, 0)
        )

    def inside(start):
        at = row * (2 * OWN) + start + jnp.where(low_lanes((1, PAIR)), 0, 1)
        return col_mask[...] * one_hot((at >= 0) & (at < rows * 2 * OWN))

    def lrelu(v):
        return jnp.where(v > 0, v, 0.1 * v)

    def realign(upper_of, lower_of):
        mixed = jnp.where(
            low_lanes(upper_of.shape), lower_of.astype(F32), upper_of.astype(F32)
        )
        return pltpu.roll(mixed, 64, 1).astype(BF16)

    def lift_first(at):
        for j in at:
            v = conv((xf1,), k_prop.at[pl.ds(0, 256)], j)
            lift1[j] = (lrelu(v) * inside(2 * j - 9)).astype(BF16)

    receive_all(ex_first, (0,))
    lift_first(range(HALO_A, HALO_A + OWN - 1))
    receive_all(ex_first, (1,))
    for copy in ex_second:
        copy.start()
    lift_first((1, 2, 3, 4, 8, 9, 10, 11))
    receive_all(ex_first, (2,))
    lift_first((0, 12))
    for j in range(12):
        v = conv((lift1,), k_middle, j)
        inner1[j] = (jnp.maximum(v, 0.0) * inside(2 * j - 8)).astype(BF16)
    for j in range(11):
        v = conv((inner1,), k_output, j) + lift1[j + 1].astype(F32)
        state1[j] = (v * inside(2 * j - 7)).astype(BF16)

    for m in range(8):
        e1[m] = realign(state1[m + 1], state1[m + 2])
    for copy in ex_state:
        copy.start()

    for copy in ex_second:
        copy.wait_recv()
    for j in range(11):
        xo2[j] = realign(xf2[j], xf2[j + 1])
    for j in range(10):
        v = conv((xo2, state1), k_prop, j)
        lift2[j] = (lrelu(v) * inside(2 * j - 6)).astype(BF16)
    for j in range(9):
        v = conv((lift2,), k_middle, j)
        inner2[j] = (jnp.maximum(v, 0.0) * inside(2 * j - 5)).astype(BF16)
    for j in range(8):
        v = conv((inner2,), k_output, j) + lift2[j + 1].astype(F32)
        s2[j] = (v * inside(2 * j - 4)).astype(BF16)

    receive_all(ex_cot)
    for j in range(7):
        v = conv((cb,), k_head_t, j)
        grad_ref[j] = (v * inside(2 * j - 3)).astype(BF16)
    for j in range(6):
        grad_in_pre[j] = conv((grad_ref,), k_second_t, j) * inside(2 * j - 2)

    for copy in ex_state:
        copy.wait_recv()
    for j in range(7):
        v = conv((s1, s2), k_merge, j)
        sigma = jax.nn.sigmoid(v)
        merged[j] = (v * sigma * inside(2 * j - 3)).astype(BF16)
        if 1 <= j <= 5:
            slope_m[j - 1] = sigma * (1.0 + v * (1.0 - sigma)) * inside(2 * j - 3)
    for j in range(6):
        v = conv((merged,), k_first, j)
        sigma = jax.nn.sigmoid(v)
        rec_inner[j] = (v * sigma * inside(2 * j - 2)).astype(BF16)
        grad_in[j] = (grad_in_pre[j] * (sigma * (1.0 + v * (1.0 - sigma)))).astype(BF16)
    for j in range(5):
        v = conv((rec_inner,), k_second, j) + merged[j + 1].astype(F32)
        refined[j] = (v * inside(2 * j - 1)).astype(BF16)
    for j in range(4):
        v = conv((refined,), k_head, j)[RIM : RIM + COLS].T
        high = v.astype(BF16)
        low = (v - high.astype(F32)).astype(BF16)
        for r in range(2):
            for i in range(4):
                piece = slice((r * 4 + i) * 16, (r * 4 + i + 1) * 16)
                at = (slice((2 * j + r) * 16, (2 * j + r + 1) * 16), slice(i * 128, (i + 1) * 128))
                z_hi[at] = high[piece]
                z_lo[at] = low[piece]
    m_at, n_at = iota((96, 128), 0), iota((96, 128), 1)
    gather = one_hot(
        (((m_at >> 2) & 7) == (n_at >> 4)) & (((m_at >> 5) * 4 + (m_at & 3)) == (n_at & 15))
    ).astype(BF16)
    total = None
    for z in (z_hi, z_lo):
        ordered = jnp.dot(gather, z[...], preferred_element_type=F32).astype(BF16)
        part = jnp.dot(ordered, shuffle[...], preferred_element_type=F32)
        total = part if total is None else total + part
    up_out[...] = total

    for j in range(5):
        v = conv((grad_in,), k_first_t, j) + grad_ref[j + 1].astype(F32)
        grad_pre[j] = (v * slope_m[j]).astype(BF16)
    for j in range(4):
        v = conv((grad_pre,), k_merge_t, j)
        for r in range(2):
            adj_out[pl.ds(2 * j + r, 128, stride=8), :] = v[
                RIM : RIM + COLS, r * 128 : (r + 1) * 128
            ].T

    for copies in (ex_first, ex_cot):
        sent_all(copies)
    for copy in ex_second + ex_state:
        copy.wait_send()


def hand_over(up_in, adj_in, up_out, adj_out, sem):
    copies = [pltpu.make_async_copy(up_in, up_out, sem.at[0])]
    for k in range(4):
        part = pl.ds(k * 256, 256)
        copies.append(pltpu.make_async_copy(adj_in.at[part], adj_out.at[part], sem.at[1 + k]))
    for copy in copies:
        copy.start()
    for copy in copies:
        copy.wait()


def on_device(
    rows,
    cols,
    features,
    prop_input,
    prop_middle,
    prop_output,
    merge_weight,
    first_weight,
    second_weight,
    head_weight,
    cotangent,
):
    def taps(weight):
        return jnp.transpose(weight, (2, 3, 0, 1))

    def vmem(*shape, dtype=BF16):
        return pltpu.VMEM(shape, dtype)

    def act(pairs, dtype=BF16):
        return pltpu.VMEM((pairs, WIDE, PAIR), dtype)

    scratch = (
        [
            vmem(2, 512, 128),
            vmem(3, 3, 64, 128),
            vmem(3, 3, 64, 64),
            vmem(3, 3, 64, 64),
            vmem(3, 3, 64, 128),
            vmem(3, 3, 64, 64),
            vmem(3, 3, 64, 64),
            vmem(3, 3, 48, 64),
            vmem(96, 512),
            vmem(512, 128, dtype=F32),
            act(OWN + 2 * HALO_A),
            act(OWN + 2 * HALO_B),
            act(11),
            act(OWN + 2 * HALO_C),
            act(8),
            act(8),
            act(13),
            act(12),
            act(11),
            act(10),
            act(9),
            act(8),
            act(7),
            act(5, F32),
            act(6),
            act(5),
            act(7),
            act(6, F32),
            act(6),
            act(5),
        ]
        + [vmem(512, 384), vmem(256, 384), vmem(256, 384), vmem(512, 384)]
        + [vmem(256, 384) for _ in range(6)]
        + [
            vmem(256, 768),
            vmem(3, 3, 64, 64, dtype=F32),
            vmem(512, 512),
            vmem(128, 512),
            vmem(128, 512),
            vmem(WIDE, PAIR, dtype=F32),
            pltpu.SemaphoreType.DMA((10,)),
            pltpu.SemaphoreType.DMA((4, len(AROUND))),
            pltpu.SemaphoreType.DMA((4, len(AROUND))),
        ]
    )
    up, adj = pl.pallas_call(
        functools.partial(kernel, rows, cols),
        out_shape=(pltpu.VMEM((96, 512), F32), pltpu.VMEM((1024, 128), F32)),
        in_specs=[pl.BlockSpec(memory_space=pl.ANY)] * 9,
        out_specs=(
            pl.BlockSpec(memory_space=pltpu.VMEM),
            pl.BlockSpec(memory_space=pltpu.VMEM),
        ),
        scratch_shapes=scratch,
        compiler_params=pltpu.CompilerParams(
            collective_id=0, has_side_effects=True, vmem_limit_bytes=60 * 1024 * 1024
        ),
    )(
        features.reshape(2, 512, 128),
        taps(prop_input[0]),
        taps(prop_middle[0]),
        taps(prop_output[0]),
        taps(merge_weight),
        taps(first_weight),
        taps(second_weight),
        taps(head_weight),
        cotangent.reshape(96, 512),
    )
    up, adj = pl.pallas_call(
        hand_over,
        out_shape=(
            jax.ShapeDtypeStruct((96, 512), F32),
            jax.ShapeDtypeStruct((1024, 128), F32),
        ),
        in_specs=[pl.BlockSpec(memory_space=pltpu.VMEM)] * 2,
        out_specs=(pl.BlockSpec(memory_space=pl.ANY), pl.BlockSpec(memory_space=pl.ANY)),
        scratch_shapes=[pltpu.SemaphoreType.DMA((5,))],
    )(*(pltpu.with_memory_space_constraint(a, pltpu.VMEM) for a in (up, adj)))
    return up.reshape(1, 3, 32, 512), adj.reshape(1, 128, 8, 128)


def solution(mesh):
    rows, cols = mesh.shape["row"], mesh.shape["col"]
    placed = (
        P(None, None, "row", "col"),
        P("section", None, None, None, None),
        P("section", None, None, None, None),
        P("section", None, None, None, None),
        P(),
        P(),
        P(),
        P(),
        P("section", None, "row", "col"),
    )
    return jax.shard_map(
        functools.partial(on_device, rows, cols),
        mesh=mesh,
        in_specs=placed,
        out_specs=(P("section", None, "row", "col"), P("section", None, "row", "col")),
        check_vma=False,
    )
```
